256 devices in a mesh: section: 8 (over x_lo, y), dp: 32 (over x_hi, z, core).
Axes of the slice: x: 4 (x_hi: 2, x_lo: 2; x = x_hi * 2 + x_lo), y: 4, z: 8, core: 2. Of those that a mesh axis runs over, the one named last changes fastest.
Arguments:
- features: bfloat16 [2, 32, 16, 16, 256], P(None, 'dp'), may hold values from -6 to 6
- timesteps: int32 [2, 32], P(None, 'dp'), may hold values from 0 to 999
- codes: bfloat16 [8, 2, 2304, 256], P('section', None, 'dp'), may hold values from -0.125 to 0.125
- scales: float32 [8, 2, 18, 2], P('section'), may hold values from 0.5 to 2
- time_weight: bfloat16 [8, 256, 512], P('section'), may hold values from -0.375 to 0.375
Outputs:
- block_outputs: bfloat16 [8, 2, 32, 16, 16, 256], P('section', None, 'dp')
The draws below stay inside these ranges and needn't reach their ends.
All inputs are finite; a program needn't handle non-finite values.
Results may differ from the reference program's by a relative error of at most 0.017.
Values may be sent and summed in bfloat16 or wider, within the bound.
No kernel may reach another device: no remote copies, remote signals or barrier semaphores. Data moves between devices by JAX's collectives and lax.ppermute only.
A program may use at most 64 MiB of HBM per device.

```python
import math
import jax
import jax.numpy as jnp
from jax import lax

CH = 256
GROUPS = 32
QB = 128
HT = 16
WT = 16
MICRO = 2
SAMPLES = 32
N_SECTION = 8


def place_ends(result, stream_key, least, top_value):
    longest = result.shape.index(max(result.shape))
    spots = []
    for shift in (0, 1):
        where = [jax.random.randint(jax.random.fold_in(stream_key, axis), (), 0, length) for axis, length in enumerate(result.shape)]
        where[longest] = (where[longest] + shift) % result.shape[longest]
        spots.append(tuple(where))
    return result.at[spots[0]].set(least).at[spots[1]].set(top_value)


def steps_of(stream_key, dims, split, smallest, largest):
    factor_of = 1.0
    for dim, parts in split:
        steps = jax.random.uniform(jax.random.fold_in(jax.random.fold_in(stream_key, 6), dim), (parts,), jnp.float32, smallest / len(split), largest / len(split))
        factor_of = factor_of * jnp.repeat(jnp.exp(steps), dims[dim] // parts).reshape((-1,) + (1,) * (len(dims) - 1 - dim))
    return factor_of


def normal_values(stream_key, dims, spread, bound, pieces=(), kind=jnp.bfloat16):
    entries = spread * jax.random.normal(stream_key, dims, jnp.float32)
    if pieces:
        entries = entries * steps_of(stream_key, dims, pieces, -0.22, 0.18)
    return jnp.clip(entries, -bound, bound).astype(kind)


def setup_inputs(seed: int = 0) -> dict:
    key_list = jax.random.split(jax.random.key(seed), 6)
    features = normal_values(key_list[0], (MICRO, SAMPLES, HT, WT, CH), 1.0, 6.0, ((1, 32),))
    timesteps = place_ends(jax.random.randint(key_list[1], (MICRO, SAMPLES), 0, 1000), jax.random.fold_in(key_list[1], 1), 0, 999).astype(jnp.int32)
    codes = normal_values(key_list[2], (N_SECTION, 2, 9 * CH, CH), (9 * CH) ** -0.5, 0.125, ((0, 8), (2, 32)))
    scales = jnp.clip(jnp.exp(math.log(2.0) - 1.3862944 * jax.random.uniform(key_list[3], (N_SECTION, 2, 9 * CH // QB, CH // QB), jnp.float32) ** steps_of(key_list[3], (N_SECTION, 2, 9 * CH // QB, CH // QB), ((0, 8),), -0.2, 0.2)), 0.5, 2.0)
    time_weight = normal_values(key_list[4], (N_SECTION, CH, 2 * CH), CH ** -0.5, 0.375, ((0, 8),))
    return {"features": features, "timesteps": timesteps, "codes": codes, "scales": scales, "time_weight": time_weight}


def sinusoid(steps_in, channels):
    half_point = channels // 2
    freqs = jnp.exp(-math.log(10000.0) * jnp.arange(half_point, dtype=jnp.float32) / half_point)
    angles = steps_in.astype(jnp.float32)[:, None] * freqs[None, :]
    return jnp.concatenate([jnp.cos(angles), jnp.sin(angles)], axis=-1)

def group_norm(values, groups):
    samples_n, height, width_px, channels = values.shape
    grouped = values.reshape(samples_n, height * width_px, groups, channels // groups)
    mean_val = lax.optimization_barrier(jnp.mean(grouped, axis=(1, 3), keepdims=True))
    centred = grouped - mean_val
    var_val = lax.optimization_barrier(jnp.mean(centred * centred, axis=(1, 3), keepdims=True))
    return (centred * lax.rsqrt(var_val + 1e-05)).reshape(samples_n, height, width_px, channels)

def patches(activation):
    samples_n, height, width_px, channels = activation.shape
    padded = jnp.pad(activation, ((0, 0), (1, 1), (1, 1), (0, 0)))
    taps = [padded[:, row_off:row_off + height, col_off:col_off + width_px, :] for row_off in range(3) for col_off in range(3)]
    return jnp.concatenate(taps, axis=-1).reshape(samples_n * height * width_px, 9 * channels)

def dequant(code_block, scale_block):
    scale_full = jnp.repeat(jnp.repeat(scale_block, QB, axis=-2), QB, axis=-1)
    return (code_block.astype(jnp.float32) * scale_full).astype(jnp.bfloat16)

def res_block(block_in, w_first, w_second, t_weight, embedding):
    samples_n, height, width_px, channels = block_in.shape
    first_in = jax.nn.silu(group_norm(block_in, GROUPS)).astype(jnp.bfloat16)
    hidden = jnp.dot(patches(first_in), w_first, preferred_element_type=jnp.float32).reshape(block_in.shape)
    emb_act = jax.nn.silu(embedding).astype(jnp.bfloat16)
    modulation = jnp.dot(emb_act, t_weight, preferred_element_type=jnp.float32)
    scale_mod = modulation[:, :channels][:, None, None, :]
    shift_mod = modulation[:, channels:][:, None, None, :]
    second_in = jax.nn.silu(group_norm(hidden, GROUPS) * (1.0 + scale_mod) + shift_mod).astype(jnp.bfloat16)
    branch = jnp.dot(patches(second_in), w_second, preferred_element_type=jnp.float32).reshape(block_in.shape)
    return (block_in + branch).astype(jnp.bfloat16)

def reference(features, timesteps, codes, scales, time_weight):
    rescale = 0.7071067811865476
    half_point = N_SECTION // 2
    weights = [dequant(codes[section_no], scales[section_no]) for section_no in range(N_SECTION)]
    results = [[None] * MICRO for section_no in range(N_SECTION)]
    for micro_no in range(MICRO):
        embedding = sinusoid(timesteps[micro_no], CH)
        entering = features[micro_no]
        for section_no in range(N_SECTION):
            if section_no < half_point:
                block_in = entering.astype(jnp.float32)
            else:
                skip_in = results[N_SECTION - 1 - section_no][micro_no]
                block_in = (entering.astype(jnp.float32) + skip_in.astype(jnp.float32)) * rescale
            block_out = res_block(block_in, weights[section_no][0], weights[section_no][1], time_weight[section_no], embedding)
            results[section_no][micro_no] = block_out
            entering = block_out
    return jnp.stack([jnp.stack(row_list, axis=0) for row_list in results], axis=0)
```

```python
import functools
import math

import jax
import jax.numpy as jnp
from jax import lax
from jax.experimental import pallas as pl
from jax.experimental.pallas import tpu as pltpu
from jax.sharding import PartitionSpec as P

GROUP = 8
QB = 128
SIDE = 16
RING = 8
RESCALE = 0.7071067811865476
VMEM = pl.BlockSpec(memory_space=pltpu.VMEM)
SMEM = pl.BlockSpec(memory_space=pltpu.SMEM)


def across_lanes(values, bit):
    lane = lax.broadcasted_iota(jnp.int32, values.shape, 1)
    return jnp.take_along_axis(values, lane ^ bit, axis=1)


def normalize(values):
    pixels, channels = values.shape
    mean = jnp.sum(values, axis=0, keepdims=True) * (1.0 / pixels)
    spread = values - mean
    square = jnp.sum(spread * spread, axis=0, keepdims=True)
    upper = lax.broadcasted_iota(jnp.int32, (8, channels), 0) < 4
    both = jnp.where(upper, mean, square)
    count = pixels
    for bit in (1, 2, 4):
        halves = [across_lanes(both[:, k : k + 128], bit) for k in range(0, channels, 128)]
        partner = jnp.concatenate(halves, axis=1)
        apart = both - partner
        between = pltpu.roll(apart * apart, 4, 0) * (0.5 * count)
        both = jnp.where(upper, 0.5 * (both + partner), both + partner + between)
        count = 2 * count
    return values - both[0:1], lax.rsqrt(both[4:5] * (1.0 / count) + 1e-05)


def silu(values):
    half = 0.5 * values
    return half + half * jnp.tanh(half)


def conv(activation, rows, weight):
    pixels, channels = activation.shape
    rows[pl.ds(SIDE, pixels), :] = activation.astype(jnp.bfloat16)
    sides = []
    for right in (0, 2, 1):
        total = None
        for down in range(3):
            tap = 3 * down + right
            part = jnp.dot(
                rows[pl.ds(SIDE * down, pixels), :],
                weight[pl.ds(channels * tap, channels), :],
                preferred_element_type=jnp.float32,
            )
            total = part if total is None else total + part
        sides.append(total)
    column = lax.broadcasted_iota(jnp.int32, activation.shape, 0) & (SIDE - 1)
    before = jnp.where(column == 0, 0.0, pltpu.roll(sides[0], 1, 0))
    after = jnp.where(column == SIDE - 1, 0.0, pltpu.roll(sides[1], pixels - 1, 0))
    return sides[2] + before + after


def block_kernel(step, entering, skip, modulation, weights, old, out, rows):
    depth = weights.shape[0] // 2
    channels = entering.shape[1]

    @pl.when(lax.axis_index("section") == step)
    def _():
        edge = jnp.zeros((SIDE, channels), jnp.bfloat16)
        rows[pl.ds(0, SIDE), :] = edge
        rows[pl.ds(rows.shape[0] - SIDE, SIDE), :] = edge
        block_in = entering[...].astype(jnp.float32)
        if skip is not None:
            block_in = (block_in + skip[...].astype(jnp.float32)) * RESCALE
        centred, inverse = normalize(block_in)
        hidden = conv(silu(centred * inverse), rows, weights.at[pl.ds(0, depth), :])
        centred, inverse = normalize(hidden)
        scale = modulation[:, :channels]
        shift = modulation[:, channels:]
        second = silu(centred * (inverse * (1.0 + scale)) + shift)
        branch = conv(second, rows, weights.at[pl.ds(depth, depth), :])
        out[...] = (block_in + branch).astype(jnp.bfloat16)


def res_block(step, entering, skip, modulation, weights, old):
    pixels, channels = entering.shape
    return pl.pallas_call(
        functools.partial(block_kernel, step),
        out_shape=jax.ShapeDtypeStruct(entering.shape, jnp.bfloat16),
        in_specs=[VMEM, None if skip is None else VMEM, VMEM, VMEM, VMEM],
        out_specs=VMEM,
        input_output_aliases={3 if skip is None else 4: 0},
        scratch_shapes=[pltpu.VMEM((pixels + 2 * SIDE, channels), jnp.bfloat16)],
        compiler_params=pltpu.CompilerParams(vmem_limit_bytes=16 * 1024 * 1024),
        cost_estimate=pl.CostEstimate(
            flops=2 * weights.shape[0] * channels * pixels,
            bytes_accessed=3000000,
            transcendentals=2 * pixels * channels,
        ),
    )(entering, skip, modulation, weights, old)


def sinusoid(steps_in, channels):
    half_point = channels // 2
    freqs = jnp.exp(-math.log(10000.0) * jnp.arange(half_point, dtype=jnp.float32) / half_point)
    angles = steps_in.astype(jnp.float32)[:, None] * freqs[None, :]
    return jnp.concatenate([jnp.cos(angles), jnp.sin(angles)], axis=-1)


def dp_place():
    position = lax.axis_index("dp")
    return position // (2 * RING), position // 2 % RING, position % 2


def assemble_kernel(there, chips, scales, mine, theirs, half, half_other, old, out):
    far, along, core = dp_place()
    ahead = 1 - 2 * core
    rows, channels = out.shape[1] // (2 * RING), out.shape[2]
    row = lax.broadcasted_iota(jnp.int32, (rows, channels), 0)

    def place(block, facing, where, number):
        side = 1 - far if facing else far
        position = lax.rem(where + RING, RING)
        first = side * (scales.shape[1] // 2) + position
        here = scales[number, pl.ds(first, 1), :]
        later = scales[number, pl.ds(first + 1, 1), :]
        scale = jnp.where(row < QB - SIDE * position, here, later)
        start = pl.multiple_of(side * (RING * rows) + position * rows, SIDE)
        scaled = (block.astype(jnp.float32) * scale).astype(jnp.bfloat16)
        out[number, pl.ds(start, rows), :] = scaled

    convs = out.shape[0]

    def spread(block, facing, where):
        for number in range(block.shape[0]):
            if number < convs:
                place(block[number], facing, where, number)
            elif block.shape[0] == 2 * convs:
                place(block[number], not facing, where, number - convs)

    for (facing, hops), block in zip(there, mine):
        spread(block, facing, along + ahead * hops)
    for (facing, hops), block in zip(there[len(there) - len(theirs) :], theirs):
        spread(block, facing, along - ahead * hops)
    if half is None:
        half, half_other = mine[-1].at[convs], theirs[-1].at[convs]
    place(half[...], chips, along + RING // 2, core)
    place(half_other[...], chips, along + RING // 2, 1 - core)


def assembled(there, facing, scales, mine, theirs, half, half_other, old):
    rows, channels = mine[0].shape[1:]
    shape = (scales.shape[0], 2 * RING * rows, channels)
    return pl.pallas_call(
        functools.partial(assemble_kernel, there, facing),
        out_shape=jax.ShapeDtypeStruct(shape, jnp.bfloat16),
        in_specs=[
            VMEM,
            [VMEM] * len(mine),
            [VMEM] * len(theirs),
            None if half is None else VMEM,
            None if half is None else VMEM,
            None if old is None else VMEM,
        ],
        out_specs=VMEM,
        input_output_aliases={} if old is None else {1 + len(mine) + len(theirs): 0},
        compiler_params=pltpu.CompilerParams(vmem_limit_bytes=16 * 1024 * 1024),
    )(scales, mine, theirs, half, half_other, old)


def gathered_weights(codes, scales, features, timesteps):
    count = lax.axis_size("dp")
    _, _, core = dp_place()
    convs, rows, channels = codes.shape

    def onward(i, hops):
        step = hops * (2 * (i % 2) - 1)
        return i // (2 * RING) * 2 * RING + (i // 2 + step) % RING * 2 + i % 2

    def along_ring(value, hops):
        return lax.ppermute(value, "dp", [(i, onward(i, hops)) for i in range(count)])

    def facing_side(value):
        return lax.ppermute(value, "dp", [(i, i ^ (2 * RING)) for i in range(count)])

    def other_core(value):
        return lax.ppermute(value, "dp", [(i, i ^ 1) for i in range(count)])

    def merged(mine, theirs):
        axis = mine.ndim - 2
        even = jnp.where(core == 0, mine, theirs)
        odd = jnp.where(core == 0, theirs, mine)
        return jnp.concatenate([even, odd], axis=axis)

    own = merged(codes, other_core(codes))
    part = jnp.where(core == 0, own[0], own[1])
    facing = facing_side(own)
    third = along_ring(own, 3)
    far_part = along_ring(part, RING // 2)
    column = jnp.concatenate([own, facing])
    far_part, third, column, scales, features, timesteps = lax.optimization_barrier(
        (far_part, third, column, scales, features, timesteps)
    )
    first = along_ring(column, 1)
    second = along_ring(column, 2)
    late = facing_side(jnp.concatenate([third, far_part[None]]))
    wide = jnp.repeat(jnp.pad(scales, ((0, 0), (0, 1), (0, 0))), QB, axis=2)
    weights = assembled(
        [(False, 0), (False, 3)],
        False,
        wide,
        [column, third],
        [other_core(third)],
        far_part,
        other_core(far_part),
        None,
    )
    weights = assembled(
        [(False, 1), (False, 2), (True, 3)],
        True,
        wide,
        [first, second, late],
        [other_core(first), other_core(second), other_core(late)],
        None,
        None,
        weights,
    )
    return weights.reshape(-1, channels), features, timesteps


def route(step, sections):
    half = sections // 2
    if step == half - 1:
        return [(s, sections - 1 - s) for s in range(sections)]
    pairs = {s: s ^ 1 for s in range(sections)}
    if step % 2:
        first = step // half * half
        pairs.update({first + k: first + (k + 1) % half for k in range(half)})
    return list(pairs.items())


def shards(features, timesteps, codes, scales, time_weight):
    sections = lax.axis_size("section")
    micros = features.shape[0]
    channels = features.shape[4]
    pixels = SIDE * SIDE
    half = sections // 2
    weights, features, timesteps = gathered_weights(codes[0], scales[0], features, timesteps)
    embedding = jax.nn.silu(sinusoid(timesteps[:, 0], channels)).astype(jnp.bfloat16)
    modulation = jnp.dot(embedding, time_weight[0], preferred_element_type=jnp.float32)
    entering = [features[m].reshape(pixels, channels) for m in range(micros)]
    outs = list(entering)
    skips = None
    for step in range(sections):
        sent = []
        for m in range(micros):
            skip = None if step < half else entering[m] if step == half else skips[m]
            outs[m] = res_block(step, entering[m], skip, modulation[m : m + 1], weights, outs[m])
            if step < sections - 1:
                sent.append(lax.ppermute(outs[m], "section", route(step, sections)))
        if step == half - 1:
            skips = sent
        entering = sent
    return jnp.stack(outs).reshape((1, micros, 1, SIDE, SIDE, channels))


def solution(mesh):
    in_specs = (
        P(None, "dp", None, None, None),
        P(None, "dp"),
        P("section", None, "dp", None),
        P("section", None, None, None),
        P("section", None, None),
    )
    out_specs = P("section", None, "dp", None, None, None)
    return jax.shard_map(shards, mesh=mesh, in_specs=in_specs, out_specs=out_specs, check_vma=False)
```

```python
import functools
import math

import jax
import jax.numpy as jnp
from jax import lax
from jax.experimental import pallas as pl
from jax.experimental.pallas import tpu as pltpu
from jax.sharding import PartitionSpec as P

GROUP = 8
QB = 128
SIDE = 16
RING = 8
RESCALE = 0.7071067811865476
VMEM = pl.BlockSpec(memory_space=pltpu.VMEM)
SMEM = pl.BlockSpec(memory_space=pltpu.SMEM)


def across_lanes(values, bit):
    lane = lax.broadcasted_iota(jnp.int32, values.shape, 1)
    return jnp.take_along_axis(values, lane ^ bit, axis=1)


def normalize(values):
    pixels, channels = values.shape
    origin = values[0:1]
    moved = values - origin
    total = jnp.sum(moved, axis=0, keepdims=True) * (1.0 / pixels)
    square = jnp.sum(moved * moved, axis=0, keepdims=True) - total * total * pixels
    means = []
    squares = []
    for k in range(0, channels, 128):
        mean = jnp.broadcast_to((origin + total)[:, k : k + 128], (8, 128))
        spread = jnp.broadcast_to(square[:, k : k + 128], (8, 128))
        count = pixels
        for bit in (1, 2, 4):
            other = across_lanes(mean, bit)
            apart = mean - other
            spread = spread + across_lanes(spread, bit) + apart * apart * (0.5 * count)
            mean = 0.5 * (mean + other)
            count = 2 * count
        means.append(mean[0:1])
        squares.append(spread[0:1])
    variance = jnp.maximum(jnp.concatenate(squares, axis=1) * (1.0 / count), 0.0)
    return values - jnp.concatenate(means, axis=1), lax.rsqrt(variance + 1e-05)


def silu(values):
    half = 0.5 * values
    return half + half * jnp.tanh(half)


def conv(activation, rows, weight):
    pixels, channels = activation.shape
    rows[pl.ds(SIDE, pixels), :] = activation.astype(jnp.bfloat16)
    sides = []
    for right in (0, 2, 1):
        total = None
        for down in range(3):
            tap = 3 * down + right
            part = jnp.dot(
                rows[pl.ds(SIDE * down, pixels), :],
                weight[pl.ds(channels * tap, channels), :],
                preferred_element_type=jnp.float32,
            )
            total = part if total is None else total + part
        sides.append(total)
    column = lax.broadcasted_iota(jnp.int32, activation.shape, 0) & (SIDE - 1)
    before = jnp.where(column == 0, 0.0, pltpu.roll(sides[0], 1, 0))
    after = jnp.where(column == SIDE - 1, 0.0, pltpu.roll(sides[1], pixels - 1, 0))
    return sides[2] + before + after


def block_kernel(step, entering, skip, modulation, weights, old, out, rows):
    depth = weights.shape[0] // 2
    channels = entering.shape[1]

    @pl.when(lax.axis_index("section") == step)
    def _():
        edge = jnp.zeros((SIDE, channels), jnp.bfloat16)
        rows[pl.ds(0, SIDE), :] = edge
        rows[pl.ds(rows.shape[0] - SIDE, SIDE), :] = edge
        block_in = entering[...].astype(jnp.float32)
        if skip is not None:
            block_in = (block_in + skip[...].astype(jnp.float32)) * RESCALE
        centred, inverse = normalize(block_in)
        hidden = conv(silu(centred * inverse), rows, weights.at[pl.ds(0, depth), :])
        centred, inverse = normalize(hidden)
        scale = modulation[:, :channels]
        shift = modulation[:, channels:]
        second = silu(centred * (inverse * (1.0 + scale)) + shift)
        branch = conv(second, rows, weights.at[pl.ds(depth, depth), :])
        out[...] = (block_in + branch).astype(jnp.bfloat16)


def res_block(step, entering, skip, modulation, weights, old):
    pixels, channels = entering.shape
    return pl.pallas_call(
        functools.partial(block_kernel, step),
        out_shape=jax.ShapeDtypeStruct(entering.shape, jnp.bfloat16),
        in_specs=[VMEM, None if skip is None else VMEM, VMEM, VMEM, VMEM],
        out_specs=VMEM,
        input_output_aliases={3 if skip is None else 4: 0},
        scratch_shapes=[pltpu.VMEM((pixels + 2 * SIDE, channels), jnp.bfloat16)],
        compiler_params=pltpu.CompilerParams(vmem_limit_bytes=16 * 1024 * 1024),
        cost_estimate=pl.CostEstimate(
            flops=2 * weights.shape[0] * channels * pixels,
            bytes_accessed=3000000,
            transcendentals=2 * pixels * channels,
        ),
    )(entering, skip, modulation, weights, old)


def sinusoid(steps_in, channels):
    half_point = channels // 2
    freqs = jnp.exp(-math.log(10000.0) * jnp.arange(half_point, dtype=jnp.float32) / half_point)
    angles = steps_in.astype(jnp.float32)[:, None] * freqs[None, :]
    return jnp.concatenate([jnp.cos(angles), jnp.sin(angles)], axis=-1)


def dp_place():
    position = lax.axis_index("dp")
    return position // (2 * RING), position // 2 % RING, position % 2


def assemble_kernel(there, chips, scales, mine, theirs, half, half_other, old, out):
    far, along, core = dp_place()
    ahead = 1 - 2 * core
    rows, channels = out.shape[1] // (2 * RING), out.shape[2]
    row = lax.broadcasted_iota(jnp.int32, (rows, channels), 0)

    def place(block, facing, where, number):
        side = 1 - far if facing else far
        position = lax.rem(where + RING, RING)
        first = side * (scales.shape[1] // 2) + position
        here = scales[number, pl.ds(first, 1), :]
        later = scales[number, pl.ds(first + 1, 1), :]
        scale = jnp.where(row < QB - SIDE * position, here, later)
        start = pl.multiple_of(side * (RING * rows) + position * rows, SIDE)
        scaled = (block.astype(jnp.float32) * scale).astype(jnp.bfloat16)
        out[number, pl.ds(start, rows), :] = scaled

    convs = out.shape[0]

    def spread(block, facing, where):
        for number in range(block.shape[0]):
            if number < convs:
                place(block[number], facing, where, number)
            elif block.shape[0] == 2 * convs:
                place(block[number], not facing, where, number - convs)

    for (facing, hops), block in zip(there, mine):
        spread(block, facing, along + ahead * hops)
    for (facing, hops), block in zip(there[len(there) - len(theirs) :], theirs):
        spread(block, facing, along - ahead * hops)
    if half is None:
        half, half_other = mine[-1].at[convs], theirs[-1].at[convs]
    place(half[...], chips, along + RING // 2, core)
    place(half_other[...], chips, along + RING // 2, 1 - core)


def assembled(there, facing, scales, mine, theirs, half, half_other, old):
    rows, channels = mine[0].shape[1:]
    shape = (scales.shape[0], 2 * RING * rows, channels)
    return pl.pallas_call(
        functools.partial(assemble_kernel, there, facing),
        out_shape=jax.ShapeDtypeStruct(shape, jnp.bfloat16),
        in_specs=[
            VMEM,
            [VMEM] * len(mine),
            [VMEM] * len(theirs),
            None if half is None else VMEM,
            None if half is None else VMEM,
            None if old is None else VMEM,
        ],
        out_specs=VMEM,
        input_output_aliases={} if old is None else {1 + len(mine) + len(theirs): 0},
        compiler_params=pltpu.CompilerParams(vmem_limit_bytes=16 * 1024 * 1024),
    )(scales, mine, theirs, half, half_other, old)


def gathered_weights(codes, scales, features, timesteps):
    count = lax.axis_size("dp")
    _, _, core = dp_place()
    convs, rows, channels = codes.shape

    def onward(i, hops):
        step = hops * (2 * (i % 2) - 1)
        return i // (2 * RING) * 2 * RING + (i // 2 + step) % RING * 2 + i % 2

    def along_ring(value, hops):
        return lax.ppermute(value, "dp", [(i, onward(i, hops)) for i in range(count)])

    def facing_side(value):
        return lax.ppermute(value, "dp", [(i, i ^ (2 * RING)) for i in range(count)])

    def other_core(value):
        return lax.ppermute(value, "dp", [(i, i ^ 1) for i in range(count)])

    def merged(mine, theirs):
        axis = mine.ndim - 2
        even = jnp.where(core == 0, mine, theirs)
        odd = jnp.where(core == 0, theirs, mine)
        return jnp.concatenate([even, odd], axis=axis)

    own = merged(codes, other_core(codes))
    part = jnp.where(core == 0, own[0], own[1])
    facing = facing_side(own)
    third = along_ring(own, 3)
    second = along_ring(own, 2)
    far_part = along_ring(part, RING // 2)
    column = jnp.concatenate([own, facing])
    far_part, third, second, column, scales, features, timesteps = lax.optimization_barrier(
        (far_part, third, second, column, scales, features, timesteps)
    )
    first = along_ring(column, 1)
    facing_second = along_ring(column[convs:], 2)
    late = facing_side(jnp.concatenate([third, far_part[None]]))
    wide = jnp.repeat(jnp.pad(scales, ((0, 0), (0, 1), (0, 0))), QB, axis=2)
    weights = assembled(
        [(False, 0), (False, 2), (False, 3)],
        False,
        wide,
        [column, second, third],
        [other_core(second), other_core(third)],
        far_part,
        other_core(far_part),
        None,
    )
    weights = assembled(
        [(False, 1), (True, 2), (True, 3)],
        True,
        wide,
        [first, facing_second, late],
        [other_core(first), other_core(facing_second), other_core(late)],
        None,
        None,
        weights,
    )
    return weights.reshape(-1, channels), features, timesteps


def route(step, sections):
    half = sections // 2
    if step == half - 1:
        return [(s, sections - 1 - s) for s in range(sections)]
    pairs = {s: s ^ 1 for s in range(sections)}
    if step % 2:
        first = step // half * half
        pairs.update({first + k: first + (k + 1) % half for k in range(half)})
    return list(pairs.items())


def shards(features, timesteps, codes, scales, time_weight):
    sections = lax.axis_size("section")
    micros = features.shape[0]
    channels = features.shape[4]
    pixels = SIDE * SIDE
    half = sections // 2
    weights, features, timesteps = gathered_weights(codes[0], scales[0], features, timesteps)
    embedding = jax.nn.silu(sinusoid(timesteps[:, 0], channels)).astype(jnp.bfloat16)
    modulation = jnp.dot(embedding, time_weight[0], preferred_element_type=jnp.float32)
    entering = [features[m].reshape(pixels, channels) for m in range(micros)]
    outs = list(entering)
    skips = None
    for step in range(sections):
        sent = []
        for m in range(micros):
            skip = None if step < half else entering[m] if step == half else skips[m]
            outs[m] = res_block(step, entering[m], skip, modulation[m : m + 1], weights, outs[m])
            if step < sections - 1:
                sent.append(lax.ppermute(outs[m], "section", route(step, sections)))
        if step == half - 1:
            skips = sent
        entering = sent
    return jnp.stack(outs).reshape((1, micros, 1, SIDE, SIDE, channels))


def solution(mesh):
    in_specs = (
        P(None, "dp", None, None, None),
        P(None, "dp"),
        P("section", None, "dp", None),
        P("section", None, None, None),
        P("section", None, None),
    )
    out_specs = P("section", None, "dp", None, None, None)
    return jax.shard_map(shards, mesh=mesh, in_specs=in_specs, out_specs=out_specs, check_vma=False)
```

```python
import functools
import math

import jax
import jax.numpy as jnp
from jax import lax
from jax.experimental import pallas as pl
from jax.experimental.pallas import tpu as pltpu
from jax.sharding import PartitionSpec as P

GROUP = 8
QB = 128
SIDE = 16
RING = 8
RESCALE = 0.7071067811865476
VMEM = pl.BlockSpec(memory_space=pltpu.VMEM)
SMEM = pl.BlockSpec(memory_space=pltpu.SMEM)


def across_lanes(values, lanes_of):
    lane = lax.broadcasted_iota(jnp.int32, values.shape, 1)
    return jnp.take_along_axis(values, lanes_of(lane), axis=1)


def group_stats(values):
    pixels, channels = values.shape
    halves = range(0, channels, 128)
    top = jnp.broadcast_to(values[0:1], (8, channels))
    origin = [across_lanes(top[:, k : k + 128], lambda lane: lane & ~(GROUP - 1)) for k in halves]
    origin = jnp.concatenate(origin, axis=1)[0:1]
    moved = values - origin
    total = jnp.sum(moved, axis=0, keepdims=True)
    square = jnp.sum(moved * moved, axis=0, keepdims=True)
    upper = lax.broadcasted_iota(jnp.int32, (8, channels), 0) < 4
    both = jnp.where(upper, total, square)
    sums = []
    for k in halves:
        half = both[:, k : k + 128]
        parts = [half]
        parts += [across_lanes(half, lambda lane, bit=bit: lane ^ bit) for bit in range(1, GROUP)]
        while len(parts) > 1:
            parts = [left + right for left, right in zip(parts[::2], parts[1::2])]
        sums += parts
    sums = jnp.concatenate(sums, axis=1) * (1.0 / (pixels * GROUP))
    mean = sums[0:1]
    variance = jnp.maximum(sums[4:5] - mean * mean, 0.0)
    return origin + mean, lax.rsqrt(variance + 1e-05)


def silu_of_twice(half):
    return half + half * jnp.tanh(half)


def conv(activation, rows, weight):
    pixels, channels = activation.shape
    rows[pl.ds(SIDE, pixels), :] = activation.astype(jnp.bfloat16)
    sides = []
    for right in (0, 2, 1):
        total = None
        for down in range(3):
            tap = 3 * down + right
            part = jnp.dot(
                rows[pl.ds(SIDE * down, pixels), :],
                weight[pl.ds(channels * tap, channels), :],
                preferred_element_type=jnp.float32,
            )
            total = part if total is None else total + part
        sides.append(total)
    column = lax.broadcasted_iota(jnp.int32, activation.shape, 0) & (SIDE - 1)
    before = jnp.where(column == 0, 0.0, pltpu.roll(sides[0], 1, 0))
    after = jnp.where(column == SIDE - 1, 0.0, pltpu.roll(sides[1], pixels - 1, 0))
    return sides[2] + before + after


def block_kernel(step, entering, skip, modulation, weights, old, out, rows):
    depth = weights.shape[0] // 2
    channels = entering.shape[1]

    @pl.when(lax.axis_index("section") == step)
    def _():
        edge = jnp.zeros((SIDE, channels), jnp.bfloat16)
        rows[pl.ds(0, SIDE), :] = edge
        rows[pl.ds(rows.shape[0] - SIDE, SIDE), :] = edge
        block_in = entering[...].astype(jnp.float32)
        if skip is not None:
            block_in = (block_in + skip[...].astype(jnp.float32)) * RESCALE
        mean, inverse = group_stats(block_in)
        first = silu_of_twice((block_in - mean) * (0.5 * inverse))
        hidden = conv(first, rows, weights.at[pl.ds(0, depth), :])
        mean, inverse = group_stats(hidden)
        scale = modulation[:, :channels]
        shift = modulation[:, channels:]
        gain = (0.5 * inverse) * (1.0 + scale)
        second = silu_of_twice((hidden - mean) * gain + 0.5 * shift)
        branch = conv(second, rows, weights.at[pl.ds(depth, depth), :])
        out[...] = (block_in + branch).astype(jnp.bfloat16)


def res_block(step, entering, skip, modulation, weights, old):
    pixels, channels = entering.shape
    return pl.pallas_call(
        functools.partial(block_kernel, step),
        out_shape=jax.ShapeDtypeStruct(entering.shape, jnp.bfloat16),
        in_specs=[VMEM, None if skip is None else VMEM, VMEM, VMEM, VMEM],
        out_specs=VMEM,
        input_output_aliases={3 if skip is None else 4: 0},
        scratch_shapes=[pltpu.VMEM((pixels + 2 * SIDE, channels), jnp.bfloat16)],
        compiler_params=pltpu.CompilerParams(vmem_limit_bytes=16 * 1024 * 1024),
        cost_estimate=pl.CostEstimate(
            flops=2 * weights.shape[0] * channels * pixels,
            bytes_accessed=3000000,
            transcendentals=2 * pixels * channels,
        ),
    )(entering, skip, modulation, weights, old)


def sinusoid(steps_in, channels):
    half_point = channels // 2
    freqs = jnp.exp(-math.log(10000.0) * jnp.arange(half_point, dtype=jnp.float32) / half_point)
    angles = steps_in.astype(jnp.float32)[:, None] * freqs[None, :]
    return jnp.concatenate([jnp.cos(angles), jnp.sin(angles)], axis=-1)


def dp_place():
    position = lax.axis_index("dp")
    return position // (2 * RING), position // 2 % RING, position % 2


def assemble_kernel(there, chips, scales, mine, theirs, half, half_other, old, out):
    far, along, core = dp_place()
    ahead = 1 - 2 * core
    rows, channels = out.shape[1] // (2 * RING), out.shape[2]
    row = lax.broadcasted_iota(jnp.int32, (rows, channels), 0)

    def place(block, facing, where, number):
        side = 1 - far if facing else far
        position = lax.rem(where + RING, RING)
        first = side * (scales.shape[1] // 2) + position
        here = scales[number, pl.ds(first, 1), :]
        later = scales[number, pl.ds(first + 1, 1), :]
        scale = jnp.where(row < QB - SIDE * position, here, later)
        start = pl.multiple_of(side * (RING * rows) + position * rows, SIDE)
        scaled = (block.astype(jnp.float32) * scale).astype(jnp.bfloat16)
        out[number, pl.ds(start, rows), :] = scaled

    convs = out.shape[0]

    def spread(block, facing, where):
        for number in range(block.shape[0]):
            if number < convs:
                place(block[number], facing, where, number)
            elif block.shape[0] == 2 * convs:
                place(block[number], not facing, where, number - convs)

    for (facing, hops), block in zip(there, mine):
        spread(block, facing, along + ahead * hops)
    for (facing, hops), block in zip(there[len(there) - len(theirs) :], theirs):
        spread(block, facing, along - ahead * hops)
    if half is None:
        half, half_other = mine[-1].at[convs], theirs[-1].at[convs]
    place(half[...], chips, along + RING // 2, core)
    place(half_other[...], chips, along + RING // 2, 1 - core)


def assembled(there, facing, scales, mine, theirs, half, half_other, old):
    rows, channels = mine[0].shape[1:]
    shape = (scales.shape[0], 2 * RING * rows, channels)
    return pl.pallas_call(
        functools.partial(assemble_kernel, there, facing),
        out_shape=jax.ShapeDtypeStruct(shape, jnp.bfloat16),
        in_specs=[
            VMEM,
            [VMEM] * len(mine),
            [VMEM] * len(theirs),
            None if half is None else VMEM,
            None if half is None else VMEM,
            None if old is None else VMEM,
        ],
        out_specs=VMEM,
        input_output_aliases={} if old is None else {1 + len(mine) + len(theirs): 0},
        compiler_params=pltpu.CompilerParams(vmem_limit_bytes=16 * 1024 * 1024),
    )(scales, mine, theirs, half, half_other, old)


def gathered_weights(codes, scales, features, timesteps):
    count = lax.axis_size("dp")
    _, _, core = dp_place()
    convs, rows, channels = codes.shape

    def onward(i, hops):
        step = hops * (2 * (i % 2) - 1)
        return i // (2 * RING) * 2 * RING + (i // 2 + step) % RING * 2 + i % 2

    def along_ring(value, hops):
        return lax.ppermute(value, "dp", [(i, onward(i, hops)) for i in range(count)])

    def facing_side(value):
        return lax.ppermute(value, "dp", [(i, i ^ (2 * RING)) for i in range(count)])

    def other_core(value):
        return lax.ppermute(value, "dp", [(i, i ^ 1) for i in range(count)])

    def merged(mine, theirs):
        axis = mine.ndim - 2
        even = jnp.where(core == 0, mine, theirs)
        odd = jnp.where(core == 0, theirs, mine)
        return jnp.concatenate([even, odd], axis=axis)

    own = merged(codes, other_core(codes))
    part = jnp.where(core == 0, own[0], own[1])
    facing = facing_side(own)
    third = along_ring(own, 3)
    second = along_ring(own, 2)
    far_part = along_ring(part, RING // 2)
    column = jnp.concatenate([own, facing])
    far_part, third, second, column, scales, features, timesteps = lax.optimization_barrier(
        (far_part, third, second, column, scales, features, timesteps)
    )
    first = along_ring(column, 1)
    facing_second = along_ring(column[convs:], 2)
    late = facing_side(jnp.concatenate([third, far_part[None]]))
    wide = jnp.repeat(jnp.pad(scales, ((0, 0), (0, 1), (0, 0))), QB, axis=2)
    weights = assembled(
        [(False, 0), (False, 2), (False, 3)],
        False,
        wide,
        [column, second, third],
        [other_core(second), other_core(third)],
        far_part,
        other_core(far_part),
        None,
    )
    weights = assembled(
        [(False, 1), (True, 2), (True, 3)],
        True,
        wide,
        [first, facing_second, late],
        [other_core(first), other_core(facing_second), other_core(late)],
        None,
        None,
        weights,
    )
    return weights.reshape(-1, channels), features, timesteps


def route(step, sections, count):
    half = sections // 2
    partner = {step: step + 1, step + 1: step}
    if step == half - 1:
        partner.update({half - 2: half + 1, half + 1: half - 2})
    if step == half:
        partner.update({s: sections - 1 - s for s in range(sections) if s < half - 2 or s > half + 1})
    pairs = []
    for s in range(sections):
        for d in range(count):
            other = (partner[s], d) if s in partner else (s, d ^ 1)
            pairs.append((s * count + d, other[0] * count + other[1]))
    return pairs


def shards(features, timesteps, codes, scales, time_weight):
    sections = lax.axis_size("section")
    count = lax.axis_size("dp")
    micros = features.shape[0]
    channels = features.shape[4]
    pixels = SIDE * SIDE
    half = sections // 2
    weights, features, timesteps = gathered_weights(codes[0], scales[0], features, timesteps)
    embedding = jax.nn.silu(sinusoid(timesteps[:, 0], channels)).astype(jnp.bfloat16)
    modulation = jnp.dot(embedding, time_weight[0], preferred_element_type=jnp.float32)
    entering = [features[m].reshape(pixels, channels) for m in range(micros)]
    outs = list(entering)
    near = far = None
    for step in range(sections):
        sent = []
        for m in range(micros):
            skip = None
            if step >= half:
                skip = (entering, near, far)[min(step - half, 2)][m]
            outs[m] = res_block(step, entering[m], skip, modulation[m : m + 1], weights, outs[m])
            if step < sections - 1:
                sent.append(lax.ppermute(outs[m], ("section", "dp"), route(step, sections, count)))
        if step == half - 1:
            near = sent
        if step == half:
            far = sent
        entering = sent
    return jnp.stack(outs).reshape((1, micros, 1, SIDE, SIDE, channels))


def solution(mesh):
    in_specs = (
        P(None, "dp", None, None, None),
        P(None, "dp"),
        P("section", None, "dp", None),
        P("section", None, None, None),
        P("section", None, None),
    )
    out_specs = P("section", None, "dp", None, None, None)
    return jax.shard_map(shards, mesh=mesh, in_specs=in_specs, out_specs=out_specs, check_vma=False)
```

```python
import functools
import math

import jax
import jax.numpy as jnp
from jax import lax
from jax.experimental import pallas as pl
from jax.experimental.pallas import tpu as pltpu
from jax.sharding import PartitionSpec as P

GROUP = 8
QB = 128
SIDE = 16
RING = 8
RESCALE = 0.7071067811865476
VMEM = pl.BlockSpec(memory_space=pltpu.VMEM)
SMEM = pl.BlockSpec(memory_space=pltpu.SMEM)


def across_lanes(values, lanes_of):
    lane = lax.broadcasted_iota(jnp.int32, values.shape, 1)
    return jnp.take_along_axis(values, lanes_of(lane), axis=1)


def group_stats(values):
    pixels, channels = values.shape
    halves = range(0, channels, 128)
    top = jnp.broadcast_to(values[0:1], (8, channels))
    origin = [across_lanes(top[:, k : k + 128], lambda lane: lane & ~(GROUP - 1)) for k in halves]
    origin = jnp.concatenate(origin, axis=1)[0:1]
    moved = values - origin
    total = jnp.sum(moved, axis=0, keepdims=True)
    square = jnp.sum(moved * moved, axis=0, keepdims=True)
    upper = lax.broadcasted_iota(jnp.int32, (8, channels), 0) < 4
    both = jnp.where(upper, total, square)
    sums = []
    for k in halves:
        half = both[:, k : k + 128]
        parts = [half]
        parts += [across_lanes(half, lambda lane, bit=bit: lane ^ bit) for bit in range(1, GROUP)]
        while len(parts) > 1:
            parts = [left + right for left, right in zip(parts[::2], parts[1::2])]
        sums += parts
    sums = jnp.concatenate(sums, axis=1) * (1.0 / (pixels * GROUP))
    mean = sums[0:1]
    variance = jnp.maximum(sums[4:5] - mean * mean, 0.0)
    return origin + mean, lax.rsqrt(variance + 1e-05)


def silu_of_twice(half):
    return half + half * jnp.tanh(half)


def conv(activation, rows, weight):
    pixels, channels = activation.shape
    rows[pl.ds(SIDE, pixels), :] = activation.astype(jnp.bfloat16)
    sides = []
    for right in (0, 2, 1):
        total = None
        for down in range(3):
            tap = 3 * down + right
            part = jnp.dot(
                rows[pl.ds(SIDE * down, pixels), :],
                weight[pl.ds(channels * tap, channels), :],
                preferred_element_type=jnp.float32,
            )
            total = part if total is None else total + part
        sides.append(total)
    column = lax.broadcasted_iota(jnp.int32, activation.shape, 0) & (SIDE - 1)
    before = jnp.where(column == 0, 0.0, pltpu.roll(sides[0], 1, 0))
    after = jnp.where(column == SIDE - 1, 0.0, pltpu.roll(sides[1], pixels - 1, 0))
    return sides[2] + before + after


def block_kernel(step, entering, skip, modulation, weights, old, out, rows):
    depth = weights.shape[0] // 2
    channels = entering.shape[1]

    @pl.when(lax.axis_index("section") == step)
    def _():
        edge = jnp.zeros((SIDE, channels), jnp.bfloat16)
        rows[pl.ds(0, SIDE), :] = edge
        rows[pl.ds(rows.shape[0] - SIDE, SIDE), :] = edge
        block_in = entering[...].astype(jnp.float32)
        if skip is not None:
            block_in = (block_in + skip[...].astype(jnp.float32)) * RESCALE
        mean, inverse = group_stats(block_in)
        first = silu_of_twice((block_in - mean) * (0.5 * inverse))
        hidden = conv(first, rows, weights.at[pl.ds(0, depth), :])
        mean, inverse = group_stats(hidden)
        scale = modulation[:, :channels]
        shift = modulation[:, channels:]
        gain = (0.5 * inverse) * (1.0 + scale)
        second = silu_of_twice((hidden - mean) * gain + 0.5 * shift)
        branch = conv(second, rows, weights.at[pl.ds(depth, depth), :])
        out[...] = (block_in + branch).astype(jnp.bfloat16)


def res_block(step, entering, skip, modulation, weights, old):
    pixels, channels = entering.shape
    return pl.pallas_call(
        functools.partial(block_kernel, step),
        out_shape=jax.ShapeDtypeStruct(entering.shape, jnp.bfloat16),
        in_specs=[VMEM, None if skip is None else VMEM, VMEM, VMEM, VMEM],
        out_specs=VMEM,
        input_output_aliases={3 if skip is None else 4: 0},
        scratch_shapes=[pltpu.VMEM((pixels + 2 * SIDE, channels), jnp.bfloat16)],
        compiler_params=pltpu.CompilerParams(vmem_limit_bytes=16 * 1024 * 1024),
        cost_estimate=pl.CostEstimate(
            flops=2 * weights.shape[0] * channels * pixels,
            bytes_accessed=3000000,
            transcendentals=2 * pixels * channels,
        ),
    )(entering, skip, modulation, weights, old)


def sinusoid(steps_in, channels):
    half_point = channels // 2
    freqs = jnp.exp(-math.log(10000.0) * jnp.arange(half_point, dtype=jnp.float32) / half_point)
    angles = steps_in.astype(jnp.float32)[:, None] * freqs[None, :]
    return jnp.concatenate([jnp.cos(angles), jnp.sin(angles)], axis=-1)


def dp_place():
    position = lax.axis_index("dp")
    return position // (2 * RING), position // 2 % RING, position % 2


def assemble_kernel(there, scales, mine, theirs, old, out):
    far, along, core = dp_place()
    ahead = 1 - 2 * core
    rows, channels = out.shape[1] // (2 * RING), out.shape[2]
    convs = out.shape[0]
    row = lax.broadcasted_iota(jnp.int32, (rows, channels), 0)

    def place(block, facing, where, number):
        side = 1 - far if facing else far
        position = lax.rem(where + RING, RING)
        first = side * (scales.shape[1] // 2) + position
        here = scales[number, pl.ds(first, 1), :]
        later = scales[number, pl.ds(first + 1, 1), :]
        scale = jnp.where(row < QB - SIDE * position, here, later)
        start = pl.multiple_of(side * (RING * rows) + position * rows, SIDE)
        scaled = (block.astype(jnp.float32) * scale).astype(jnp.bfloat16)
        out[number, pl.ds(start, rows), :] = scaled

    def spread(block, facing, hops, half):
        count = block.shape[0]
        for n in range(count - count % 2):
            place(block[n], facing if count == convs else n >= convs, along + hops, n % convs)
        if count % 2:
            place(block[count - 1], facing, along + RING // 2, half)

    for (facing, hops), block in zip(there, mine):
        spread(block, facing, ahead * hops, core)
    for (facing, hops), block in zip(there[len(there) - len(theirs) :], theirs):
        spread(block, facing, -ahead * hops, 1 - core)


def assembled(there, scales, mine, theirs, old):
    rows, channels = mine[0].shape[1:]
    shape = (scales.shape[0], 2 * RING * rows, channels)
    return pl.pallas_call(
        functools.partial(assemble_kernel, there),
        out_shape=jax.ShapeDtypeStruct(shape, jnp.bfloat16),
        in_specs=[VMEM, [VMEM] * len(mine), [VMEM] * len(theirs), None if old is None else VMEM],
        out_specs=VMEM,
        input_output_aliases={} if old is None else {1 + len(mine) + len(theirs): 0},
        compiler_params=pltpu.CompilerParams(vmem_limit_bytes=16 * 1024 * 1024),
    )(scales, mine, theirs, old)


def gathered_weights(codes, scales, features, timesteps):
    count = lax.axis_size("dp")
    _, _, core = dp_place()

    def onward(i, hops):
        step = hops * (2 * (i % 2) - 1)
        return i // (2 * RING) * 2 * RING + (i // 2 + step) % RING * 2 + i % 2

    def along_ring(value, hops):
        return lax.ppermute(value, "dp", [(i, onward(i, hops)) for i in range(count)])

    def facing_side(value):
        return lax.ppermute(value, "dp", [(i, i ^ (2 * RING)) for i in range(count)])

    def other_core(value):
        return lax.ppermute(value, "dp", [(i, i ^ 1) for i in range(count)])

    def one_conv(value):
        return jnp.where(core == 0, value[0:1], value[1:2])

    other = other_core(codes)
    even = jnp.where(core == 0, codes, other)
    odd = jnp.where(core == 0, other, codes)
    own = jnp.concatenate([even, odd], axis=1)
    facing = facing_side(own)
    third = along_ring(own, 3)
    second = along_ring(own, 2)
    column = jnp.concatenate([own, facing, one_conv(third)])
    third, second, column, scales, features, timesteps = lax.optimization_barrier(
        (third, second, column, scales, features, timesteps)
    )
    first = along_ring(column, 1)
    facing_second = along_ring(column[2:4], 2)
    facing_third = facing_side(third)
    wide = jnp.repeat(jnp.pad(scales, ((0, 0), (0, 1), (0, 0))), QB, axis=2)
    weights = assembled(
        [(False, 0), (False, 2), (False, 3)],
        wide,
        [column[:4], second, third],
        [other_core(second), other_core(third)],
        None,
    )
    last = along_ring(one_conv(facing_third), 1)
    there = [(False, 1), (True, 2), (True, 3)]
    mine = [first, facing_second, facing_third]
    weights = assembled(there, wide, mine, [other_core(block) for block in mine], weights)
    weights = assembled([(True, 4)], wide, [last], [other_core(last)], weights)
    return weights.reshape(-1, weights.shape[2]), features, timesteps


def route(step, sections, count):
    half = sections // 2
    partner = {step: step + 1, step + 1: step}
    if step == half - 1:
        partner.update({half - 2: half + 1, half + 1: half - 2})
    if step == half:
        partner.update({s: sections - 1 - s for s in range(sections) if s < half - 2 or s > half + 1})
    pairs = []
    for s in range(sections):
        for d in range(count):
            other = (partner[s], d) if s in partner else (s, d ^ 1)
            pairs.append((s * count + d, other[0] * count + other[1]))
    return pairs


def shards(features, timesteps, codes, scales, time_weight):
    sections = lax.axis_size("section")
    count = lax.axis_size("dp")
    micros = features.shape[0]
    channels = features.shape[4]
    pixels = SIDE * SIDE
    half = sections // 2
    weights, features, timesteps = gathered_weights(codes[0], scales[0], features, timesteps)
    embedding = jax.nn.silu(sinusoid(timesteps[:, 0], channels)).astype(jnp.bfloat16)
    modulation = jnp.dot(embedding, time_weight[0], preferred_element_type=jnp.float32)
    entering = [features[m].reshape(pixels, channels) for m in range(micros)]
    outs = list(entering)
    near = far = None
    for step in range(sections):
        sent = []
        for m in range(micros):
            skip = None
            if step >= half:
                skip = (entering, near, far)[min(step - half, 2)][m]
            outs[m] = res_block(step, entering[m], skip, modulation[m : m + 1], weights, outs[m])
            if step < sections - 1:
                sent.append(lax.ppermute(outs[m], ("section", "dp"), route(step, sections, count)))
        if step == half - 1:
            near = sent
        if step == half:
            far = sent
        entering = sent
    return jnp.stack(outs).reshape((1, micros, 1, SIDE, SIDE, channels))


def solution(mesh):
    in_specs = (
        P(None, "dp", None, None, None),
        P(None, "dp"),
        P("section", None, "dp", None),
        P("section", None, None, None),
        P("section", None, None),
    )
    out_specs = P("section", None, "dp", None, None, None)
    return jax.shard_map(shards, mesh=mesh, in_specs=in_specs, out_specs=out_specs, check_vma=False)
```

```python
import functools
import math

import jax
import jax.numpy as jnp
from jax import lax
from jax.experimental import pallas as pl
from jax.experimental.pallas import tpu as pltpu
from jax.sharding import PartitionSpec as P

GROUP = 8
QB = 128
SIDE = 16
RING = 8
RESCALE = 0.7071067811865476
VMEM = pl.BlockSpec(memory_space=pltpu.VMEM)
SMEM = pl.BlockSpec(memory_space=pltpu.SMEM)


def across_lanes(values, lanes_of):
    lane = lax.broadcasted_iota(jnp.int32, values.shape, 1)
    return jnp.take_along_axis(values, lanes_of(lane), axis=1)


def group_stats(values):
    pixels, channels = values.shape
    halves = range(0, channels, 128)
    top = jnp.broadcast_to(values[0:1], (8, channels))
    origin = [across_lanes(top[:, k : k + 128], lambda lane: lane & ~(GROUP - 1)) for k in halves]
    origin = jnp.concatenate(origin, axis=1)[0:1]
    moved = values - origin
    total = jnp.sum(moved, axis=0, keepdims=True)
    square = jnp.sum(moved * moved, axis=0, keepdims=True)
    upper = lax.broadcasted_iota(jnp.int32, (8, channels), 0) < 4
    both = jnp.where(upper, total, square)
    sums = []
    for k in halves:
        half = both[:, k : k + 128]
        parts = [half]
        parts += [across_lanes(half, lambda lane, bit=bit: lane ^ bit) for bit in range(1, GROUP)]
        while len(parts) > 1:
            parts = [left + right for left, right in zip(parts[::2], parts[1::2])]
        sums += parts
    sums = jnp.concatenate(sums, axis=1) * (1.0 / (pixels * GROUP))
    mean = sums[0:1]
    variance = jnp.maximum(sums[4:5] - mean * mean, 0.0)
    return origin + mean, lax.rsqrt(variance + 1e-05)


def silu_of_twice(half):
    return half + half * jnp.tanh(half)


def conv(activation, rows, weight):
    pixels, channels = activation.shape
    rows[pl.ds(SIDE, pixels), :] = activation.astype(jnp.bfloat16)
    sides = []
    for right in (0, 2, 1):
        total = None
        for down in range(3):
            tap = 3 * down + right
            part = jnp.dot(
                rows[pl.ds(SIDE * down, pixels), :],
                weight[pl.ds(channels * tap, channels), :],
                preferred_element_type=jnp.float32,
            )
            total = part if total is None else total + part
        sides.append(total)
    column = lax.broadcasted_iota(jnp.int32, activation.shape, 0) & (SIDE - 1)
    before = jnp.where(column == 0, 0.0, pltpu.roll(sides[0], 1, 0))
    after = jnp.where(column == SIDE - 1, 0.0, pltpu.roll(sides[1], pixels - 1, 0))
    return sides[2] + before + after


def block_kernel(step, entering, skip, modulation, weights, old, out, rows):
    depth = weights.shape[0] // 2
    channels = entering.shape[1]

    @pl.when(lax.axis_index("section") == step)
    def _():
        edge = jnp.zeros((SIDE, channels), jnp.bfloat16)
        rows[pl.ds(0, SIDE), :] = edge
        rows[pl.ds(rows.shape[0] - SIDE, SIDE), :] = edge
        block_in = entering[...].astype(jnp.float32)
        if skip is not None:
            block_in = (block_in + skip[...].astype(jnp.float32)) * RESCALE
        mean, inverse = group_stats(block_in)
        first = silu_of_twice((block_in - mean) * (0.5 * inverse))
        hidden = conv(first, rows, weights.at[pl.ds(0, depth), :])
        mean, inverse = group_stats(hidden)
        scale = modulation[:, :channels]
        shift = modulation[:, channels:]
        gain = (0.5 * inverse) * (1.0 + scale)
        second = silu_of_twice((hidden - mean) * gain + 0.5 * shift)
        branch = conv(second, rows, weights.at[pl.ds(depth, depth), :])
        out[...] = (block_in + branch).astype(jnp.bfloat16)


def res_block(step, entering, skip, modulation, weights, old):
    pixels, channels = entering.shape
    return pl.pallas_call(
        functools.partial(block_kernel, step),
        out_shape=jax.ShapeDtypeStruct(entering.shape, jnp.bfloat16),
        in_specs=[VMEM, None if skip is None else VMEM, VMEM, VMEM, VMEM],
        out_specs=VMEM,
        input_output_aliases={3 if skip is None else 4: 0},
        scratch_shapes=[pltpu.VMEM((pixels + 2 * SIDE, channels), jnp.bfloat16)],
        compiler_params=pltpu.CompilerParams(vmem_limit_bytes=16 * 1024 * 1024),
        cost_estimate=pl.CostEstimate(
            flops=2 * weights.shape[0] * channels * pixels,
            bytes_accessed=3000000,
            transcendentals=2 * pixels * channels,
        ),
    )(entering, skip, modulation, weights, old)


def sinusoid(steps_in, channels):
    half_point = channels // 2
    freqs = jnp.exp(-math.log(10000.0) * jnp.arange(half_point, dtype=jnp.float32) / half_point)
    angles = steps_in.astype(jnp.float32)[:, None] * freqs[None, :]
    return jnp.concatenate([jnp.cos(angles), jnp.sin(angles)], axis=-1)


def dp_place():
    position = lax.axis_index("dp")
    return position // (2 * RING), position // 2 % RING, position % 2


def assemble_kernel(there, scales, mine, theirs, old, out):
    far, along, core = dp_place()
    ahead = 1 - 2 * core
    rows, channels = out.shape[1] // (2 * RING), out.shape[2]
    convs = out.shape[0]
    row = lax.broadcasted_iota(jnp.int32, (rows, channels), 0)

    def place(block, facing, where, number):
        side = 1 - far if facing else far
        position = lax.rem(where + RING, RING)
        first = side * (scales.shape[1] // 2) + position
        here = scales[number, pl.ds(first, 1), :]
        later = scales[number, pl.ds(first + 1, 1), :]
        scale = jnp.where(row < QB - SIDE * position, here, later)
        start = pl.multiple_of(side * (RING * rows) + position * rows, SIDE)
        scaled = (block.astype(jnp.float32) * scale).astype(jnp.bfloat16)
        out[number, pl.ds(start, rows), :] = scaled

    def spread(block, facing, hops, half):
        count = block.shape[0]
        for n in range(count - count % 2):
            place(block[n], facing if count == convs else n >= convs, along + hops, n % convs)
        if count % 2:
            place(block[count - 1], facing, along + RING // 2, half)

    for (facing, hops), block in zip(there, mine):
        spread(block, facing, ahead * hops, core)
    for (facing, hops), block in zip(there[len(there) - len(theirs) :], theirs):
        spread(block, facing, -ahead * hops, 1 - core)


def assembled(there, scales, mine, theirs, old):
    rows, channels = mine[0].shape[1:]
    shape = (scales.shape[0], 2 * RING * rows, channels)
    return pl.pallas_call(
        functools.partial(assemble_kernel, there),
        out_shape=jax.ShapeDtypeStruct(shape, jnp.bfloat16),
        in_specs=[VMEM, [VMEM] * len(mine), [VMEM] * len(theirs), None if old is None else VMEM],
        out_specs=VMEM,
        input_output_aliases={} if old is None else {1 + len(mine) + len(theirs): 0},
        compiler_params=pltpu.CompilerParams(vmem_limit_bytes=16 * 1024 * 1024),
    )(scales, mine, theirs, old)


def gathered_weights(codes, scales, features, timesteps):
    count = lax.axis_size("dp")
    _, _, core = dp_place()

    def onward(i, hops):
        step = hops * (2 * (i % 2) - 1)
        return i // (2 * RING) * 2 * RING + (i // 2 + step) % RING * 2 + i % 2

    def along_ring(value, hops):
        return lax.ppermute(value, "dp", [(i, onward(i, hops)) for i in range(count)])

    def facing_side(value):
        return lax.ppermute(value, "dp", [(i, i ^ (2 * RING)) for i in range(count)])

    def other_core(value):
        return lax.ppermute(value, "dp", [(i, i ^ 1) for i in range(count)])

    def one_conv(value):
        return jnp.where(core == 0, value[0:1], value[1:2])

    other = other_core(codes)
    even = jnp.where(core == 0, codes, other)
    odd = jnp.where(core == 0, other, codes)
    own = jnp.concatenate([even, odd], axis=1)
    facing = facing_side(own)
    third = along_ring(own, 3)
    second = along_ring(own, 2)
    column = jnp.concatenate([own, facing, one_conv(third)])
    third, second, column, scales, features, timesteps = lax.optimization_barrier(
        (third, second, column, scales, features, timesteps)
    )
    first = along_ring(column, 1)
    facing_second = along_ring(column[2:4], 2)
    facing_third = facing_side(third)
    wide = jnp.repeat(jnp.pad(scales, ((0, 0), (0, 1), (0, 0))), QB, axis=2)
    weights = assembled(
        [(False, 0), (False, 2), (False, 3)],
        wide,
        [column[:4], second, third],
        [other_core(second), other_core(third)],
        None,
    )
    last = along_ring(one_conv(facing_third), 1)
    there = [(False, 1), (True, 2), (True, 3)]
    mine = [first, facing_second, facing_third]
    weights = assembled(there, wide, mine, [other_core(block) for block in mine], weights)
    weights = assembled([(True, 4)], wide, [last], [other_core(last)], weights)
    return weights.reshape(-1, weights.shape[2]), features, timesteps


def route(step, sections, count):
    half = sections // 2
    partner = {step: step + 1, step + 1: step}
    if step == half - 1:
        partner.update({half - 2: half + 1, half + 1: half - 2})
    if step == half:
        partner.update({s: sections - 1 - s for s in range(sections) if s < half - 2 or s > half + 1})
    pairs = []
    for s in range(sections):
        for d in range(count):
            other = (partner[s], d) if s in partner else (s, d ^ 1)
            pairs.append((s * count + d, other[0] * count + other[1]))
    return pairs


def shards(features, timesteps, codes, scales, time_weight):
    sections = lax.axis_size("section")
    count = lax.axis_size("dp")
    micros = features.shape[0]
    channels = features.shape[4]
    pixels = SIDE * SIDE
    half = sections // 2
    weights, features, timesteps = gathered_weights(codes[0], scales[0], features, timesteps)
    embedding = jax.nn.silu(sinusoid(timesteps[:, 0], channels)).astype(jnp.bfloat16)
    modulation = jnp.dot(embedding, time_weight[0], preferred_element_type=jnp.float32)
    entering = [features[m].reshape(pixels, channels) for m in range(micros)]
    outs = list(entering)
    near = far = None
    for step in range(sections):
        sent = []
        for m in range(micros):
            skip = None
            if step >= half:
                skip = (entering, near, far)[min(step - half, 2)][m]
            outs[m] = res_block(step, entering[m], skip, modulation[m : m + 1], weights, outs[m])
            if step < sections - 1:
                sent.append(lax.ppermute(outs[m], ("section", "dp"), route(step, sections, count)))
        if step == half - 1:
            near = sent
        if step == half:
            far = sent
        entering = sent
    whole = features.reshape(micros, pixels, channels)
    for m in range(micros):
        whole = lax.dynamic_update_index_in_dim(whole, outs[m], m, 0)
    return whole.reshape((1, micros, 1, SIDE, SIDE, channels))


def solution(mesh):
    in_specs = (
        P(None, "dp", None, None, None),
        P(None, "dp"),
        P("section", None, "dp", None),
        P("section", None, None, None),
        P("section", None, None),
    )
    out_specs = P("section", None, "dp", None, None, None)
    return jax.shard_map(shards, mesh=mesh, in_specs=in_specs, out_specs=out_specs, check_vma=False)
```
